32 devices in a mesh: row: 16 (over z, x, core), col: 2 (over y).
Axes of the slice: x: 2, y: 2, z: 4, core: 2. Of those that a mesh axis runs over, the one named last changes fastest.
Arguments:
- target_images: float32 [512, 3, 1024], P(('row', 'col')), may hold values from -6 to 6
- target_labels: int32 [512], P(('row', 'col')), may hold values from 0 to 9
- support_images: float32 [128, 3, 1024], P('col'), may hold values from -6 to 6
- support_labels: float32 [128, 10], replicated, may hold values from -3 to 3
- panel_order: int32 [128], replicated, may hold values from 0 to 127, each once
Outputs:
- loss_value: float32 [], replicated
- grad_support: float32 [128, 3, 1024], P('col')
- grad_labels: float32 [128, 10], replicated
The draws below stay inside these ranges and needn't reach their ends.
Inputs may be any that keep to these rules, and one draw needn't show every extreme that they name: `panel_order`: every support index appears exactly once.
All inputs are finite; a program needn't handle non-finite values.
Results may differ from the reference program's by a relative error of at most 0.0003.
Values sent between devices are 32-bit elements; how exact they have to be, the bound alone decides.
A program may use at most 256 MiB of HBM per device.

```python
import math
import jax
import jax.numpy as jnp
from jax import lax

SIDE = 32
PIX = 1024
CH = 3
CLASSES = 10
SUPPORT = 128
TARGETS = 512


def image_law(key, shape):
    return jnp.clip(jax.random.normal(jax.random.fold_in(key, 3), shape, jnp.float32), -6.0, 6.0)


def support_common(key):
    return image_law(jax.random.fold_in(key, 101), (SUPPORT, CH, PIX))


def target_common(key):
    support_set = support_common(key)
    base = image_law(jax.random.fold_in(key, 202), (TARGETS, CH, PIX))
    noise = jax.random.normal(jax.random.fold_in(key, 203), (TARGETS, CH, PIX), jnp.float32)
    copied = jax.random.randint(jax.random.fold_in(key, 204), (TARGETS,), 0, 4) == 0
    source = jax.random.randint(jax.random.fold_in(key, 205), (TARGETS,), 0, SUPPORT)
    row_flags = jax.random.randint(jax.random.fold_in(key, 206), (TARGETS, SIDE), 0, 2) == 1
    pixel_flags = jnp.repeat(row_flags, SIDE, axis=1)
    chosen = jnp.take(support_set, source, axis=0)
    near_copy = jnp.clip(2.0 * chosen + 0.05 * noise, -6.0, 6.0)
    selected = jnp.logical_and(copied[:, None], pixel_flags)[:, None, :]
    return jnp.where(selected, near_copy, base)


def draw_support_images(key, part):
    return support_common(key)


def draw_target_images(key, part):
    return target_common(key)


def plant(values, key, least, high):
    extent = values.shape
    index_at = [jax.random.randint(jax.random.fold_in(key, axis), (), 0, extent[axis]) for axis in range(len(extent))]
    values = values.at[tuple(index_at)].set(least)
    longest = extent.index(max(extent))
    index_at[longest] = (index_at[longest] + 1) % extent[longest]
    return values.at[tuple(index_at)].set(high)


def centred(key, extent, width, reach, kind=jnp.bfloat16):
    drawn = jax.random.normal(key, extent, jnp.float32) * width
    return jnp.minimum(jnp.maximum(drawn, -reach), reach).astype(kind)


def setup_inputs(seed: int = 0) -> dict:
    seeds = jax.random.split(jax.random.key(seed), 6)
    return {
        "target_images": draw_target_images(jax.random.fold_in(seeds[5], 71), 0),
        "target_labels": plant(jax.random.randint(seeds[1], (TARGETS,), 0, CLASSES), jax.random.fold_in(seeds[1], 1), 0, CLASSES - 1).astype(jnp.int32),
        "support_images": draw_support_images(jax.random.fold_in(seeds[5], 71), 0),
        "support_labels": centred(seeds[3], (SUPPORT, CLASSES), 0.5, 3.0, jnp.float32),
        "panel_order": jax.random.permutation(seeds[4], SUPPORT).astype(jnp.int32),
    }


JITTER = 0.1
RIDGE = 0.01

def shifted(planes, stride):
    filler = jnp.zeros(planes.shape[:-1] + (abs(stride),), planes.dtype)
    if stride > 0:
        return jnp.concatenate([planes[..., stride:], filler], axis=-1)
    return jnp.concatenate([filler, planes[..., :stride]], axis=-1)

def window(planes, side_len):
    column = jnp.arange(planes.shape[-1], dtype=jnp.int32) % side_len
    across = planes + jnp.where(column < side_len - 1, shifted(planes, 1), 0.0)
    across = across + jnp.where(column > 0, shifted(planes, -1), 0.0)
    return (across + shifted(across, side_len) + shifted(across, -side_len)) / 9.0

def rectify(covariance, first_diag, second_diag):
    scales = jnp.sqrt((first_diag + JITTER) * (second_diag + JITTER))
    cosine = covariance / scales
    angles = jnp.arccos(cosine)
    energy = scales * (jnp.sqrt(1.0 - cosine * cosine) + (math.pi - angles) * cosine) / math.pi
    return (energy, (math.pi - angles) / math.pi)

def self_maps(images, side_len):
    first_diag = window(lax.optimization_barrier(jnp.mean(images * images, axis=1)), side_len)
    energy, unused = rectify(first_diag, first_diag, first_diag)
    return (first_diag, window(energy, side_len))

def pair_kernel(first_images, second_images, first_maps, second_maps, side_len):
    products = first_images[:, None, 0] * second_images[None, :, 0]
    for channel in range(1, first_images.shape[1]):
        products = products + first_images[:, None, channel] * second_images[None, :, channel]
    first_sigma = window(products / first_images.shape[1], side_len)
    first_energy, first_slope = rectify(first_sigma, first_maps[0][:, None], second_maps[0][None, :])
    second_sigma = window(first_energy, side_len)
    tangent = window(first_energy + first_slope * first_sigma, side_len)
    second_energy, second_slope = rectify(second_sigma, first_maps[1][:, None], second_maps[1][None, :])
    return lax.optimization_barrier(jnp.mean(second_energy + second_slope * tangent, axis=-1))

def order_matrix(panel_order, blocks):
    return (panel_order[:, None] == jnp.arange(blocks, dtype=jnp.int32)[None, :]).astype(jnp.float32)

def to_stored(labels, matrix):
    return jnp.dot(matrix, labels.reshape(matrix.shape[0], -1), precision=lax.Precision.HIGHEST).reshape(labels.shape)

def to_logical(labels, matrix):
    return jnp.dot(matrix.T, labels.reshape(matrix.shape[0], -1), precision=lax.Precision.HIGHEST).reshape(labels.shape)

def ridge_factor(kernel):
    number = kernel.shape[0]
    ridge_term = RIDGE * jnp.trace(kernel) / number
    return jnp.linalg.cholesky(kernel + ridge_term * jnp.eye(number, dtype=kernel.dtype))

def ridge_solve(factor, rhs):
    middle = lax.linalg.triangular_solve(factor, rhs, left_side=True, lower=True)
    return lax.linalg.triangular_solve(factor, middle, left_side=True, lower=True, transpose_a=True)

def reference(target_images, target_labels, support_images, support_labels, panel_order):
    highest = lax.Precision.HIGHEST
    target_maps = self_maps(target_images, SIDE)
    block_rows = math.gcd(TARGETS, 32)
    block_count = TARGETS // block_rows
    image_blocks = target_images.reshape(block_count, block_rows, CH, PIX)
    first_blocks = target_maps[0].reshape(block_count, block_rows, PIX)
    second_blocks = target_maps[1].reshape(block_count, block_rows, PIX)
    support_maps = self_maps(support_images, SIDE)

    def forward_block(inputs):
        return pair_kernel(inputs[0], support_images, (inputs[1], inputs[2]), support_maps, SIDE)
    kernel_ts = lax.map(forward_block, (image_blocks, first_blocks, second_blocks)).reshape(TARGETS, SUPPORT)
    group_rows = math.gcd(SUPPORT, 16)
    groups = SUPPORT // group_rows
    positions = jnp.arange(groups, dtype=jnp.int32)

    def support_rows(position, support_set):
        rows_part = lax.dynamic_slice_in_dim(support_set, position * group_rows, group_rows, 0)
        return pair_kernel(rows_part, support_set, self_maps(rows_part, SIDE), self_maps(support_set, SIDE), SIDE)
    kernel_ss = lax.map(lambda position: support_rows(position, support_images), positions).reshape(SUPPORT, SUPPORT)
    matrix = order_matrix(panel_order, SUPPORT)
    stored_labels = to_stored(support_labels, matrix)
    factor = ridge_factor(kernel_ss)
    alphas = ridge_solve(factor, stored_labels)
    wanted = (target_labels[:, None] == jnp.arange(CLASSES, dtype=jnp.int32)[None, :]).astype(jnp.float32) - 0.1
    residual = jnp.dot(kernel_ts, alphas, precision=highest) - wanted
    loss_value = 0.5 * jnp.sum(residual * residual) / TARGETS
    alpha_grad = jnp.dot(kernel_ts.T, residual, precision=highest)
    adjoint = ridge_solve(factor, alpha_grad)
    kss_grad = -jnp.dot(adjoint, alphas.T, precision=highest) - RIDGE / SUPPORT * jnp.sum(adjoint * alphas) * jnp.eye(SUPPORT, dtype=jnp.float32)
    kts_grad = jnp.dot(residual, alphas.T, precision=highest)

    def target_step(running, inputs):
        images, first_diag, second_diag, cotangent = inputs

        def kernel_of(support_set):
            return pair_kernel(images, support_set, (first_diag, second_diag), self_maps(support_set, SIDE), SIDE)
        unused, pullback = jax.vjp(kernel_of, support_images)
        return (running + pullback(cotangent)[0], None)
    gradient = jnp.zeros((SUPPORT, CH, PIX), jnp.float32)
    gradient, unused = lax.scan(target_step, gradient, (image_blocks, first_blocks, second_blocks, kts_grad.reshape(block_count, block_rows, SUPPORT)))

    def support_step(running, position):
        cotangent = lax.dynamic_slice_in_dim(kss_grad, position * group_rows, group_rows, 0)
        unused, pullback = jax.vjp(lambda support_set: support_rows(position, support_set), support_images)
        return (running + pullback(cotangent)[0], None)
    gradient, unused = lax.scan(support_step, gradient, positions)
    return (loss_value, gradient, to_logical(adjoint, matrix))
```

```python
import functools
import math

import jax
import jax.numpy as jnp
from jax import lax
from jax.experimental import pallas as pl
from jax.experimental.pallas import tpu as pltpu
from jax.sharding import PartitionSpec as P

SIDE = 32
CLASSES = 10
JITTER = 0.1
RIDGE = 0.01
LANES = 128
SUB = 8
CHUNK = 8
MESH = pl.DeviceIdType.MESH

ACOS = (
    1.5707963050,
    -0.2145988016,
    0.0889789874,
    -0.0501743046,
    0.0308918810,
    -0.0170881256,
    0.0066700901,
    -0.0012624911,
)


def arc(cosine):
    size = jnp.abs(cosine)
    poly = jnp.full_like(size, ACOS[-1] / math.pi)
    for factor in ACOS[-2::-1]:
        poly = poly * size + factor / math.pi
    rest = 1.0 - size
    inverse_root = lax.rsqrt(rest)
    angle = rest * inverse_root * poly
    slope = jnp.where(cosine >= 0.0, 1.0 - angle, angle)
    square = rest * (1.0 + size)
    inverse_sine = lax.rsqrt(square)
    return square * inverse_sine, inverse_sine, slope


def self_energy(diag):
    scale = diag + JITTER
    sine, unused, slope = arc(diag / scale)
    return scale * sine / math.pi + slope * diag, slope + sine / math.pi


def plane_window(values):
    column = lax.broadcasted_iota(jnp.int32, values.shape, 1)
    last = values.shape[1] - 1
    across = values + jnp.where(column < last, pltpu.roll(values, last, 1), 0.0)
    across = across + jnp.where(column > 0, pltpu.roll(values, 1, 1), 0.0)
    zero = jnp.zeros_like(across[:1])
    down = jnp.concatenate([across[1:], zero], axis=0)
    up = jnp.concatenate([zero, across[:-1]], axis=0)
    return (across + down + up) * (1.0 / 9.0)


def lane_window(values):
    lane = lax.broadcasted_iota(jnp.int32, values.shape, 2)
    across = values + pltpu.roll(values, 1, 2) + pltpu.roll(values, LANES - 1, 2)
    across = jnp.where(lane < SIDE, across, 0.0)
    zero = jnp.zeros_like(across[:1])
    down = jnp.concatenate([across[1:], zero], axis=0)
    up = jnp.concatenate([zero, across[:-1]], axis=0)
    return (across + down + up) * (1.0 / 9.0)


def maps_kernel(
    first_ref, second_ref, kernel_ref, prod_ref, q1_ref, q2_ref,
    near_ref, far_ref, one_ref, two_ref, three_ref, four_ref,
):
    channels = first_ref.shape[0]
    pixels = SIDE * SIDE

    @pl.when(pl.program_id(0) == 0)
    def _():
        square = second_ref[0] * second_ref[0]
        for channel in range(1, channels):
            square = square + second_ref[channel] * second_ref[channel]
        diag = plane_window(square * (1.0 / channels))
        far_ref[0] = lax.rsqrt(diag + JITTER)
        far_ref[1] = (diag + JITTER) * lax.rsqrt(diag + JITTER)
        diag = plane_window(self_energy(diag)[0])
        far_ref[2] = lax.rsqrt(diag + JITTER)
        far_ref[3] = (diag + JITTER) * lax.rsqrt(diag + JITTER)
        for ref in (one_ref, two_ref, three_ref, four_ref):
            ref[0] = jnp.zeros(ref.shape[1:], jnp.float32)
            ref[SIDE + 1] = jnp.zeros(ref.shape[1:], jnp.float32)

            def clear(row, carry, ref=ref):
                ref[row, 0] = jnp.zeros((SUB, LANES), jnp.float32)
                ref[row, SIDE + 1] = jnp.zeros((SUB, LANES), jnp.float32)
                return carry

            lax.fori_loop(1, SIDE + 1, clear, 0)

    square = first_ref[0, 0] * first_ref[0, 0]
    for channel in range(1, channels):
        square = square + first_ref[channel, 0] * first_ref[channel, 0]
    diag = lane_window(square * (1.0 / channels))
    near_ref[0] = lax.rsqrt(diag + JITTER)
    near_ref[1] = (diag + JITTER) * lax.rsqrt(diag + JITTER)
    inside = lax.broadcasted_iota(jnp.int32, diag.shape, 2) < SIDE
    diag = lane_window(jnp.where(inside, self_energy(diag)[0], 0.0))
    near_ref[2] = lax.rsqrt(diag + JITTER)
    near_ref[3] = (diag + JITTER) * lax.rsqrt(diag + JITTER)

    def spread(ref, lead, row, start):
        block = ref[lead + (row,)]
        return jnp.stack(
            [jnp.broadcast_to(block[:, x : x + 1], (SUB, LANES)) for x in range(start, start + CHUNK)]
        )

    def across(ref, lead, row, start):
        return jnp.stack(
            [
                jnp.broadcast_to(ref[lead, row, x : x + 1, :], (SUB, LANES))
                for x in range(start, start + CHUNK)
            ]
        )

    def near(index, row, start):
        return spread(near_ref, (index,), row, start)

    def far(index, row, start):
        return across(far_ref, index, row, start)

    def box(ref, row, start):
        width = CHUNK + 2
        tall = (
            ref[row, start : start + width]
            + ref[row + 1, start : start + width]
            + ref[row + 2, start : start + width]
        )
        return tall[:CHUNK] + tall[1 : CHUNK + 1] + tall[2:]

    def put(ref, row, start, values):
        ref[row + 1, start + 1 : start + 1 + CHUNK] = values

    starts = tuple(range(0, SIDE, CHUNK))

    def products(row, carry):
        for start in starts:
            total = spread(first_ref, (0, 0), row, start) * across(second_ref, 0, row, start)
            for channel in range(1, channels):
                total = total + spread(first_ref, (channel, 0), row, start) * across(
                    second_ref, channel, row, start
                )
            put(one_ref, row, start, total)
        return carry

    lax.fori_loop(0, SIDE, products, 0)

    def first_level(row, carry):
        for start in starts:
            sigma = box(one_ref, row, start) * (1.0 / (9.0 * channels))
            cosine = sigma * (near(0, row, start) * far(0, row, start))
            sine, unused, slope = arc(cosine)
            scale = near(1, row, start) * far(1, row, start)
            bent = slope * sigma
            energy = scale * sine * (1.0 / math.pi) + bent
            put(two_ref, row, start, energy)
            put(three_ref, row, start, energy + bent)
            prod_ref[0, row, start : start + CHUNK] = cosine
            q1_ref[0, row, start : start + CHUNK] = slope
        return carry

    lax.fori_loop(0, SIDE, first_level, 0)

    def second_level(row, total):
        for start in starts:
            sigma = box(two_ref, row, start) * (1.0 / 9.0)
            tangent = box(three_ref, row, start) * (1.0 / 9.0)
            inverse = near(2, row, start) * far(2, row, start)
            scale = near(3, row, start) * far(3, row, start)
            cosine = sigma * inverse
            sine, inverse_sine, slope = arc(cosine)
            part = scale * sine * (1.0 / math.pi)
            values = part + slope * (sigma + tangent)
            turn = tangent * inverse_sine * (1.0 / math.pi)
            put(one_ref, row, start, slope)
            put(four_ref, row, start, slope + turn * inverse)
            q2_ref[0, row, start : start + CHUNK] = part - turn * cosine
            total = total + jnp.sum(values, axis=0)
        return total

    total = lax.fori_loop(0, SIDE, second_level, jnp.zeros((SUB, LANES), jnp.float32))
    kernel_ref[0] = total * (1.0 / pixels)

    def back(row, carry):
        for start in starts:
            inner = box(one_ref, row, start) * (1.0 / 9.0)
            energy = box(four_ref, row, start) * (1.0 / 9.0) + inner
            cosine = prod_ref[0, row, start : start + CHUNK]
            slope = q1_ref[0, row, start : start + CHUNK]
            scale = near(1, row, start) * far(1, row, start)
            square = (1.0 - cosine) * (1.0 + cosine)
            inverse_sine = lax.rsqrt(square)
            turn = inner * cosine * inverse_sine * (1.0 / math.pi)
            put(two_ref, row, start, (inner + energy) * slope + turn)
            q1_ref[0, row, start : start + CHUNK] = scale * (
                energy * (square * inverse_sine) * (1.0 / math.pi) - turn * cosine
            )
        return carry

    lax.fori_loop(0, SIDE, back, 0)

    def last(row, carry):
        for start in starts:
            prod_ref[0, row, start : start + CHUNK] = box(two_ref, row, start) * (
                1.0 / (9.0 * channels)
            )
        return carry

    lax.fori_loop(0, SIDE, last, 0)


def pair_maps(first, second):
    channels, groups = first.shape[:2]
    plane = pltpu.VMEM((SIDE + 2, SIDE + 2, SUB, LANES), jnp.float32)
    big = jax.ShapeDtypeStruct((groups, SIDE, SIDE, SUB, LANES), jnp.float32)
    big_spec = pl.BlockSpec((1, SIDE, SIDE, SUB, LANES), lambda g: (g, 0, 0, 0, 0))
    return pl.pallas_call(
        maps_kernel,
        grid=(groups,),
        out_shape=(jax.ShapeDtypeStruct((groups, SUB, LANES), jnp.float32), big, big, big),
        in_specs=[
            pl.BlockSpec((channels, 1, SIDE, SUB, LANES), lambda g: (0, g, 0, 0, 0)),
            pl.BlockSpec((channels, SIDE, SIDE, LANES), lambda g: (0, 0, 0, 0)),
        ],
        out_specs=(pl.BlockSpec((1, SUB, LANES), lambda g: (g, 0, 0)), big_spec, big_spec, big_spec),
        scratch_shapes=[
            pltpu.VMEM((4, SIDE, SUB, LANES), jnp.float32),
            pltpu.VMEM((4, SIDE, SIDE, LANES), jnp.float32),
            plane, plane, plane, plane,
        ],
        compiler_params=pltpu.CompilerParams(vmem_limit_bytes=58 * 1024 * 1024),
        name="pair_maps",
    )(first, second)


ROWS = 4


def contract_kernel(weight_ref, first_ref, second_ref, prod_ref, q1_ref, q2_ref, out_ref, d_ref, a_ref, b_ref):
    channels, groups = first_ref.shape[:2]
    step = pl.program_id(0)

    def body(index, carry):
        row = step * ROWS + index
        for start in range(0, SIDE, CHUNK):
            window = slice(start, start + CHUNK)
            totals = [None] * (channels + 2)

            def add(slot, value):
                totals[slot] = value if totals[slot] is None else totals[slot] + value

            for group in range(groups):
                weight = weight_ref[group][None]
                part = prod_ref[group, index, window] * weight
                for channel in range(channels):
                    block = first_ref[channel, group, row]
                    near = jnp.stack(
                        [
                            jnp.broadcast_to(block[:, x : x + 1], (SUB, LANES))
                            for x in range(start, start + CHUNK)
                        ]
                    )
                    add(channel, part * near)
                add(channels, q1_ref[group, index, window] * weight)
                add(channels + 1, q2_ref[group, index, window] * weight)
            for channel in range(channels):
                d_ref[channel, row, window, :] = jnp.sum(totals[channel], axis=1)
            a_ref[row, window, :] = jnp.sum(totals[channels], axis=1)
            b_ref[row, window, :] = jnp.sum(totals[channels + 1], axis=1)
        return carry

    lax.fori_loop(0, ROWS, body, 0)

    @pl.when(step == SIDE // ROWS - 1)
    def _():
        square = second_ref[0] * second_ref[0]
        for channel in range(1, channels):
            square = square + second_ref[channel] * second_ref[channel]
        first_diag = plane_window(square * (1.0 / channels))
        energy, rate = self_energy(first_diag)
        second_diag = plane_window(energy)
        grad_two = b_ref[...] * (0.5 / (second_diag + JITTER))
        grad_one = a_ref[...] * (0.5 / (first_diag + JITTER)) + plane_window(grad_two) * rate
        a_ref[...] = plane_window(grad_one) * (2.0 / channels)
        strips = SIDE * SIDE // LANES
        rows = SIDE // strips
        for channel in range(channels):
            for strip in range(strips):
                window = slice(strip * rows, (strip + 1) * rows)
                value = d_ref[channel, window] + a_ref[window] * second_ref[channel, window]
                out_ref[channel * strips + strip] = value.reshape(LANES, LANES).T


def contract(weight, first, second, prod, q1, q2):
    channels, groups = first.shape[:2]
    big_spec = pl.BlockSpec((groups, ROWS, SIDE, SUB, LANES), lambda s: (0, s, 0, 0, 0))
    strips = channels * SIDE * SIDE // LANES
    return pl.pallas_call(
        contract_kernel,
        grid=(SIDE // ROWS,),
        out_shape=jax.ShapeDtypeStruct((strips, LANES, LANES), jnp.float32),
        in_specs=[
            pl.BlockSpec(weight.shape, lambda s: (0, 0, 0)),
            pl.BlockSpec(first.shape, lambda s: (0, 0, 0, 0, 0)),
            pl.BlockSpec(second.shape, lambda s: (0, 0, 0, 0)),
            big_spec, big_spec, big_spec,
        ],
        out_specs=pl.BlockSpec((strips, LANES, LANES), lambda s: (0, 0, 0)),
        scratch_shapes=[
            pltpu.VMEM((channels, SIDE, SIDE, LANES), jnp.float32),
            pltpu.VMEM((SIDE, SIDE, LANES), jnp.float32),
            pltpu.VMEM((SIDE, SIDE, LANES), jnp.float32),
        ],
        compiler_params=pltpu.CompilerParams(vmem_limit_bytes=50 * 1024 * 1024),
        name="contract",
    )(weight, first, second, prod, q1, q2)


def bits_of(row_count, col_count):
    rows = row_count.bit_length() - 1
    cols = col_count.bit_length() - 1
    order = [("row", 0)] if rows else []
    return order + [("col", k) for k in range(cols)] + [("row", k) for k in range(1, rows)]


def flip(index, bit):
    size = 1 << bit
    mine = lax.rem(lax.div(index, jnp.int32(size)), jnp.int32(2))
    return mine, index + size - 2 * size * mine


def partner_of(axis, bit):
    row, col = lax.axis_index("row"), lax.axis_index("col")
    if axis == "row":
        mine, row = flip(row, bit)
    else:
        mine, col = flip(col, bit)
    return mine, (row, col)


def greet(partners):
    barrier = pltpu.get_barrier_semaphore()
    for unused, device in partners:
        pl.semaphore_signal(barrier, inc=1, device_id=device, device_id_type=MESH)
    pl.semaphore_wait(barrier, len(partners))


def sum_kernel(bits, value_ref, out_ref, send_ref, recv_ref, send_sem, recv_sem):
    partners = [partner_of(*item) for item in bits]
    greet(partners)
    total = value_ref[...]
    for step, (unused, device) in enumerate(partners):
        send_ref[step] = total
        copy = pltpu.make_async_remote_copy(
            src_ref=send_ref.at[step], dst_ref=recv_ref.at[step],
            send_sem=send_sem.at[step], recv_sem=recv_sem.at[step],
            device_id=device, device_id_type=MESH,
        )
        copy.start()
        copy.wait()
        total = total + recv_ref[step]
    out_ref[...] = total


def sum_all(value, bits, collective):
    steps = len(bits)
    return pl.pallas_call(
        functools.partial(sum_kernel, bits),
        out_shape=jax.ShapeDtypeStruct(value.shape, value.dtype),
        in_specs=[pl.BlockSpec(memory_space=pltpu.VMEM)],
        out_specs=pl.BlockSpec(memory_space=pltpu.VMEM),
        scratch_shapes=[
            pltpu.VMEM((steps,) + value.shape, value.dtype),
            pltpu.VMEM((steps,) + value.shape, value.dtype),
            pltpu.SemaphoreType.DMA((steps,)),
            pltpu.SemaphoreType.DMA((steps,)),
        ],
        compiler_params=pltpu.CompilerParams(collective_id=collective, has_side_effects=True),
        name="sum_all",
    )(value)


def gather_kernel(bits, value_ref, out_ref, hold_ref, send_sem, recv_sem):
    partners = [partner_of(*item) for item in bits]
    greet(partners)
    place = 0
    for step, (mine, unused) in enumerate(partners):
        place = place + (mine << step)
    hold_ref[place] = value_ref[...]
    for step, (unused, device) in enumerate(partners):
        size = 1 << step
        window = pl.ds(lax.div(place, jnp.int32(size)) * size, size)
        copy = pltpu.make_async_remote_copy(
            src_ref=hold_ref.at[window], dst_ref=hold_ref.at[window],
            send_sem=send_sem.at[step], recv_sem=recv_sem.at[step],
            device_id=device, device_id_type=MESH,
        )
        copy.start()
        copy.wait()
    out_ref[...] = hold_ref[...]


def gather_all(value, bits, collective):
    steps = len(bits)
    shape = (1 << steps,) + value.shape
    return pl.pallas_call(
        functools.partial(gather_kernel, bits),
        out_shape=jax.ShapeDtypeStruct(shape, value.dtype),
        in_specs=[pl.BlockSpec(memory_space=pltpu.VMEM)],
        out_specs=pl.BlockSpec(memory_space=pltpu.VMEM),
        scratch_shapes=[
            pltpu.VMEM(shape, value.dtype),
            pltpu.SemaphoreType.DMA((steps,)),
            pltpu.SemaphoreType.DMA((steps,)),
        ],
        compiler_params=pltpu.CompilerParams(collective_id=collective, has_side_effects=True),
        name="gather_all",
    )(value)


def aligned(start):
    return start if isinstance(start, int) else pl.multiple_of(start, SUB)


def reduce_kernel(bits, value_ref, out_ref, hold_ref, recv_ref, back_ref, send_sem, recv_sem, back_send, back_recv):
    strips, support = value_ref.shape[:2]
    partners = [partner_of(*item) for item in bits]
    greet(partners)
    hold_ref[...] = value_ref[...]
    lead, size = strips, support
    lead_at, size_at = 0, 0
    offset = 0
    undo = []
    cols = sum(axis == "col" for axis, unused in bits)
    for step, (axis, unused) in enumerate(bits):
        mine, device = partners[step]
        if axis == "col" or (size // 2) % SUB == 0:
            kind = 1
            half = size // 2
            keep_at, send_at = size_at + mine * half, size_at + (1 - mine) * half
            keep = (pl.ds(lead_at, lead), pl.ds(aligned(keep_at), half))
            send = (pl.ds(lead_at, lead), pl.ds(aligned(send_at), half))
        elif lead % 2 == 0:
            kind = 0
            half = lead // 2
            keep_at, send_at = lead_at + mine * half, lead_at + (1 - mine) * half
            keep = (pl.ds(keep_at, half), pl.ds(aligned(size_at), size))
            send = (pl.ds(send_at, half), pl.ds(aligned(size_at), size))
        else:
            kind = None
            keep = send = (pl.ds(lead_at, lead), pl.ds(aligned(size_at), size))
        if kind == 1:
            shape = (lead, half)
        elif kind == 0:
            shape = (half, size)
        else:
            shape = (lead, size)
        land = (pl.ds(offset, shape[0]), pl.ds(0, shape[1]))
        offset += shape[0]
        copy = pltpu.make_async_remote_copy(
            src_ref=hold_ref.at[send], dst_ref=recv_ref.at[land],
            send_sem=send_sem.at[step], recv_sem=recv_sem.at[step],
            device_id=device, device_id_type=MESH,
        )
        copy.start()
        copy.wait()
        hold_ref[keep] = hold_ref[keep] + recv_ref[land]
        if kind == 1:
            size, size_at = half, keep_at
        elif kind == 0:
            lead, lead_at = half, keep_at
        if axis == "row" and kind is not None:
            undo.append((device, keep))
    window = (pl.ds(lead_at, lead), pl.ds(aligned(size_at), size))
    back_ref[window] = hold_ref[window]
    for step, (device, keep) in enumerate(reversed(undo)):
        copy = pltpu.make_async_remote_copy(
            src_ref=back_ref.at[keep], dst_ref=back_ref.at[keep],
            send_sem=back_send.at[step], recv_sem=back_recv.at[step],
            device_id=device, device_id_type=MESH,
        )
        copy.start()
        copy.wait()
    panel = support >> cols
    start = lax.axis_index("col") * panel
    out_ref[...] = back_ref[:, pl.ds(pl.multiple_of(start, SUB), panel)]


def reduce_panels(value, row_count, col_count, collective):
    strips, support = value.shape[:2]
    rows, cols = row_count.bit_length() - 1, col_count.bit_length() - 1
    bits = [("col", k) for k in reversed(range(cols))] + [("row", k) for k in range(rows)]
    steps = len(bits)
    panel = support // col_count
    return pl.pallas_call(
        functools.partial(reduce_kernel, bits),
        out_shape=jax.ShapeDtypeStruct((strips, panel, LANES), value.dtype),
        in_specs=[pl.BlockSpec(memory_space=pltpu.VMEM)],
        out_specs=pl.BlockSpec(memory_space=pltpu.VMEM),
        scratch_shapes=[
            pltpu.VMEM(value.shape, value.dtype),
            pltpu.VMEM((strips * steps, max(support // 2, SUB), LANES), value.dtype),
            pltpu.VMEM(value.shape, value.dtype),
            pltpu.SemaphoreType.DMA((steps,)),
            pltpu.SemaphoreType.DMA((steps,)),
            pltpu.SemaphoreType.DMA((steps,)),
            pltpu.SemaphoreType.DMA((steps,)),
        ],
        compiler_params=pltpu.CompilerParams(
            collective_id=collective, has_side_effects=True, vmem_limit_bytes=40 * 1024 * 1024
        ),
        name="reduce_panels",
    )(value)


def order_matrix(panel_order, blocks):
    return (panel_order[:, None] == jnp.arange(blocks, dtype=jnp.int32)[None, :]).astype(
        jnp.float32
    )


def ridge_factor(kernel):
    number = kernel.shape[0]
    ridge_term = RIDGE * jnp.trace(kernel) / number
    return jnp.linalg.cholesky(kernel + ridge_term * jnp.eye(number, dtype=kernel.dtype))


def ridge_solve(factor, rhs):
    middle = lax.linalg.triangular_solve(factor, rhs, left_side=True, lower=True)
    return lax.linalg.triangular_solve(factor, middle, left_side=True, lower=True, transpose_a=True)


def local(target_images, target_labels, support_images, support_labels, panel_order):
    highest = lax.Precision.HIGHEST
    row_count = lax.axis_size("row")
    col_count = lax.axis_size("col")
    devices = row_count * col_count
    panel_size, channels, pixels = support_images.shape
    support = panel_size * col_count
    targets_dev = target_images.shape[0]
    bits = bits_of(row_count, col_count)
    place = 0
    for step, (axis, bit) in enumerate(bits):
        place = place + (((lax.axis_index(axis) >> bit) & 1) << step)

    gathered = lax.all_gather(support_images, "col", axis=0, tiled=True)
    own_rows = -(-support // devices)
    owners = support // own_rows
    own_start = lax.rem(place, owners) * own_rows
    own = lax.dynamic_slice_in_dim(gathered, own_start, own_rows, 0)
    count = targets_dev + own_rows
    groups = -(-count // SUB)
    first = jnp.concatenate([target_images, own], axis=0)
    first = jnp.pad(first, ((0, groups * SUB - count), (0, 0), (0, 0)))
    first = first.reshape(groups, SUB, channels, SIDE, SIDE).transpose(2, 0, 3, 1, 4)
    first = jnp.pad(first, ((0, 0),) * 4 + ((0, LANES - SIDE),))
    second = gathered.transpose(1, 2, 0).reshape(channels, SIDE, SIDE, support)

    values, prod, q1, q2 = pair_maps(first, second)
    values = values.reshape(groups * SUB, support)
    kernel_ts = values[:targets_dev]
    mine = values[targets_dev:count]
    block = jnp.pad(mine, ((0, -own_rows % SUB), (0, 0)))
    kernel_ss = gather_all(block, bits, 1)[:owners, :own_rows].reshape(support, support)

    wanted = (target_labels[:, None] == jnp.arange(CLASSES, dtype=jnp.int32)[None, :]).astype(
        jnp.float32
    ) - 0.1
    matrix = order_matrix(panel_order, support)
    stored_labels = jnp.dot(matrix, support_labels, precision=highest)
    factor = ridge_factor(kernel_ss)
    alphas = ridge_solve(factor, stored_labels)
    residual = jnp.dot(kernel_ts, alphas, precision=highest) - wanted
    partial = jnp.dot(residual.T, kernel_ts, precision=highest)
    squared = jnp.full((1, support), jnp.sum(residual * residual), jnp.float32)
    message = jnp.concatenate([partial, squared], axis=0)
    message = jnp.pad(message, ((0, -(CLASSES + 1) % SUB), (0, 0)))
    summed = sum_all(message, bits, 2)
    alpha_grad = summed[:CLASSES].T
    total_targets = targets_dev * devices
    loss_value = 0.5 * summed[CLASSES, 0] / total_targets
    adjoint = ridge_solve(factor, alpha_grad)
    own_alphas = lax.dynamic_slice_in_dim(alphas, own_start, own_rows, 0)
    own_adjoint = lax.dynamic_slice_in_dim(adjoint, own_start, own_rows, 0)
    ids = own_start + jnp.arange(own_rows, dtype=jnp.int32)
    diagonal = (ids[:, None] == jnp.arange(support, dtype=jnp.int32)[None, :]).astype(jnp.float32)
    kss_grad = (
        -jnp.dot(own_adjoint, alphas.T, precision=highest)
        - jnp.dot(own_alphas, adjoint.T, precision=highest)
        - 2.0 * RIDGE / support * jnp.sum(adjoint * alphas) * diagonal
    )
    kss_grad = jnp.where(place < owners, kss_grad, 0.0)
    kts_grad = jnp.dot(residual, alphas.T, precision=highest)
    weight = jnp.concatenate([kts_grad, kss_grad], axis=0) * (1.0 / pixels)
    weight = jnp.pad(weight, ((0, groups * SUB - count), (0, 0))).reshape(groups, SUB, support)

    gradient = contract(weight, first, second, prod, q1, q2)
    panel = reduce_panels(gradient, row_count, col_count, 3)
    grad_support = (
        panel.reshape(channels, pixels // LANES, panel_size, LANES)
        .transpose(2, 0, 1, 3)
        .reshape(panel_size, channels, pixels)
    )
    return (loss_value, grad_support, jnp.dot(matrix.T, adjoint, precision=highest))


def solution(mesh):
    placed = (P(("row", "col"), None, None), P(("row", "col")), P("col", None, None), P(), P())
    return jax.shard_map(
        local,
        mesh=mesh,
        in_specs=placed,
        out_specs=(P(), P("col", None, None), P()),
        check_vma=False,
    )
```

```python
import functools
import math

import jax
import jax.numpy as jnp
from jax import lax
from jax.experimental import pallas as pl
from jax.experimental.pallas import tpu as pltpu
from jax.sharding import PartitionSpec as P

SIDE = 32
CLASSES = 10
JITTER = 0.1
RIDGE = 0.01
LANES = 128
SUB = 8
CHUNK = 8
MESH = pl.DeviceIdType.MESH

ACOS = (
    1.5707963050,
    -0.2145988016,
    0.0889789874,
    -0.0501743046,
    0.0308918810,
    -0.0170881256,
    0.0066700901,
    -0.0012624911,
)


def arc(cosine):
    size = jnp.abs(cosine)
    poly = jnp.full_like(size, ACOS[-1] / math.pi)
    for factor in ACOS[-2::-1]:
        poly = poly * size + factor / math.pi
    rest = 1.0 - size
    inverse_root = lax.rsqrt(rest)
    angle = rest * inverse_root * poly
    slope = jnp.where(cosine >= 0.0, 1.0 - angle, angle)
    square = rest * (1.0 + size)
    inverse_sine = lax.rsqrt(square)
    return square * inverse_sine, inverse_sine, slope


def self_energy(diag):
    scale = diag + JITTER
    sine, unused, slope = arc(diag / scale)
    return scale * sine / math.pi + slope * diag, slope + sine / math.pi


def plane_window(values):
    column = lax.broadcasted_iota(jnp.int32, values.shape, 1)
    last = values.shape[1] - 1
    across = values + jnp.where(column < last, pltpu.roll(values, last, 1), 0.0)
    across = across + jnp.where(column > 0, pltpu.roll(values, 1, 1), 0.0)
    zero = jnp.zeros_like(across[:1])
    down = jnp.concatenate([across[1:], zero], axis=0)
    up = jnp.concatenate([zero, across[:-1]], axis=0)
    return (across + down + up) * (1.0 / 9.0)


def lane_window(values):
    lane = lax.broadcasted_iota(jnp.int32, values.shape, 2)
    across = values + pltpu.roll(values, 1, 2) + pltpu.roll(values, LANES - 1, 2)
    across = jnp.where(lane < SIDE, across, 0.0)
    zero = jnp.zeros_like(across[:1])
    down = jnp.concatenate([across[1:], zero], axis=0)
    up = jnp.concatenate([zero, across[:-1]], axis=0)
    return (across + down + up) * (1.0 / 9.0)


def maps_kernel(
    first_ref, second_ref, kernel_ref, prod_ref, q1_ref, q2_ref,
    near_ref, far_ref, one_ref, two_ref, three_ref, four_ref,
):
    channels = first_ref.shape[0]
    pixels = SIDE * SIDE

    @pl.when(pl.program_id(0) == 0)
    def _():
        square = second_ref[0] * second_ref[0]
        for channel in range(1, channels):
            square = square + second_ref[channel] * second_ref[channel]
        diag = plane_window(square * (1.0 / channels))
        far_ref[0] = lax.rsqrt(diag + JITTER)
        far_ref[1] = (diag + JITTER) * lax.rsqrt(diag + JITTER)
        diag = plane_window(self_energy(diag)[0])
        far_ref[2] = lax.rsqrt(diag + JITTER)
        far_ref[3] = (diag + JITTER) * lax.rsqrt(diag + JITTER)
        for ref in (one_ref, two_ref, three_ref, four_ref):
            ref[0] = jnp.zeros(ref.shape[1:], jnp.float32)
            ref[SIDE + 1] = jnp.zeros(ref.shape[1:], jnp.float32)

            def clear(row, carry, ref=ref):
                ref[row, 0] = jnp.zeros((SUB, LANES), jnp.float32)
                ref[row, SIDE + 1] = jnp.zeros((SUB, LANES), jnp.float32)
                return carry

            lax.fori_loop(1, SIDE + 1, clear, 0)

    square = first_ref[0, 0] * first_ref[0, 0]
    for channel in range(1, channels):
        square = square + first_ref[channel, 0] * first_ref[channel, 0]
    diag = lane_window(square * (1.0 / channels))
    near_ref[0] = lax.rsqrt(diag + JITTER)
    near_ref[1] = (diag + JITTER) * lax.rsqrt(diag + JITTER)
    inside = lax.broadcasted_iota(jnp.int32, diag.shape, 2) < SIDE
    diag = lane_window(jnp.where(inside, self_energy(diag)[0], 0.0))
    near_ref[2] = lax.rsqrt(diag + JITTER)
    near_ref[3] = (diag + JITTER) * lax.rsqrt(diag + JITTER)

    def spread(ref, lead, row, start):
        block = ref[lead + (row,)]
        return jnp.stack(
            [jnp.broadcast_to(block[:, x : x + 1], (SUB, LANES)) for x in range(start, start + CHUNK)]
        )

    def across(ref, lead, row, start):
        return jnp.stack(
            [
                jnp.broadcast_to(ref[lead, row, x : x + 1, :], (SUB, LANES))
                for x in range(start, start + CHUNK)
            ]
        )

    def near(index, row, start):
        return spread(near_ref, (index,), row, start)

    def far(index, row, start):
        return across(far_ref, index, row, start)

    def box(ref, row, start):
        width = CHUNK + 2
        tall = (
            ref[row, start : start + width]
            + ref[row + 1, start : start + width]
            + ref[row + 2, start : start + width]
        )
        return tall[:CHUNK] + tall[1 : CHUNK + 1] + tall[2:]

    def put(ref, row, start, values):
        ref[row + 1, start + 1 : start + 1 + CHUNK] = values

    starts = tuple(range(0, SIDE, CHUNK))

    def products(row, carry):
        for start in starts:
            total = spread(first_ref, (0, 0), row, start) * across(second_ref, 0, row, start)
            for channel in range(1, channels):
                total = total + spread(first_ref, (channel, 0), row, start) * across(
                    second_ref, channel, row, start
                )
            put(one_ref, row, start, total)
        return carry

    lax.fori_loop(0, SIDE, products, 0)

    def first_level(row, carry):
        for start in starts:
            sigma = box(one_ref, row, start) * (1.0 / (9.0 * channels))
            cosine = sigma * (near(0, row, start) * far(0, row, start))
            sine, unused, slope = arc(cosine)
            scale = near(1, row, start) * far(1, row, start)
            bent = slope * sigma
            energy = scale * sine * (1.0 / math.pi) + bent
            put(two_ref, row, start, energy)
            put(three_ref, row, start, energy + bent)
            prod_ref[0, row, start : start + CHUNK] = cosine
            q1_ref[0, row, start : start + CHUNK] = slope
        return carry

    lax.fori_loop(0, SIDE, first_level, 0)

    def second_level(row, total):
        for start in starts:
            sigma = box(two_ref, row, start) * (1.0 / 9.0)
            tangent = box(three_ref, row, start) * (1.0 / 9.0)
            inverse = near(2, row, start) * far(2, row, start)
            scale = near(3, row, start) * far(3, row, start)
            cosine = sigma * inverse
            sine, inverse_sine, slope = arc(cosine)
            part = scale * sine * (1.0 / math.pi)
            values = part + slope * (sigma + tangent)
            turn = tangent * inverse_sine * (1.0 / math.pi)
            put(one_ref, row, start, slope)
            put(four_ref, row, start, slope + turn * inverse)
            q2_ref[0, row, start : start + CHUNK] = part - turn * cosine
            total = total + jnp.sum(values, axis=0)
        return total

    total = lax.fori_loop(0, SIDE, second_level, jnp.zeros((SUB, LANES), jnp.float32))
    kernel_ref[0] = total * (1.0 / pixels)

    def back(row, carry):
        for start in starts:
            inner = box(one_ref, row, start) * (1.0 / 9.0)
            energy = box(four_ref, row, start) * (1.0 / 9.0) + inner
            cosine = prod_ref[0, row, start : start + CHUNK]
            slope = q1_ref[0, row, start : start + CHUNK]
            scale = near(1, row, start) * far(1, row, start)
            square = (1.0 - cosine) * (1.0 + cosine)
            inverse_sine = lax.rsqrt(square)
            turn = inner * cosine * inverse_sine * (1.0 / math.pi)
            put(two_ref, row, start, (inner + energy) * slope + turn)
            q1_ref[0, row, start : start + CHUNK] = scale * (
                energy * (square * inverse_sine) * (1.0 / math.pi) - turn * cosine
            )
        return carry

    lax.fori_loop(0, SIDE, back, 0)

    def last(row, carry):
        for start in starts:
            prod_ref[0, row, start : start + CHUNK] = box(two_ref, row, start) * (
                1.0 / (9.0 * channels)
            )
        return carry

    lax.fori_loop(0, SIDE, last, 0)


def pair_maps(first, second):
    channels, groups = first.shape[:2]
    plane = pltpu.VMEM((SIDE + 2, SIDE + 2, SUB, LANES), jnp.float32)
    big = jax.ShapeDtypeStruct((groups, SIDE, SIDE, SUB, LANES), jnp.float32)
    big_spec = pl.BlockSpec((1, SIDE, SIDE, SUB, LANES), lambda g: (g, 0, 0, 0, 0))
    return pl.pallas_call(
        maps_kernel,
        grid=(groups,),
        out_shape=(jax.ShapeDtypeStruct((groups, SUB, LANES), jnp.float32), big, big, big),
        in_specs=[
            pl.BlockSpec((channels, 1, SIDE, SUB, LANES), lambda g: (0, g, 0, 0, 0)),
            pl.BlockSpec((channels, SIDE, SIDE, LANES), lambda g: (0, 0, 0, 0)),
        ],
        out_specs=(pl.BlockSpec((1, SUB, LANES), lambda g: (g, 0, 0)), big_spec, big_spec, big_spec),
        scratch_shapes=[
            pltpu.VMEM((4, SIDE, SUB, LANES), jnp.float32),
            pltpu.VMEM((4, SIDE, SIDE, LANES), jnp.float32),
            plane, plane, plane, plane,
        ],
        compiler_params=pltpu.CompilerParams(vmem_limit_bytes=58 * 1024 * 1024),
        name="pair_maps",
    )(first, second)


ROWS = 4


def contract_kernel(weight_ref, first_ref, second_ref, prod_ref, q1_ref, q2_ref, out_ref, d_ref, a_ref, b_ref):
    channels, groups = first_ref.shape[:2]
    step = pl.program_id(0)

    def body(index, carry):
        row = step * ROWS + index
        for start in range(0, SIDE, CHUNK):
            window = slice(start, start + CHUNK)
            totals = [None] * (channels + 2)

            def add(slot, value):
                totals[slot] = value if totals[slot] is None else totals[slot] + value

            for group in range(groups):
                weight = weight_ref[group][None]
                part = prod_ref[group, index, window] * weight
                for channel in range(channels):
                    block = first_ref[channel, group, row]
                    near = jnp.stack(
                        [
                            jnp.broadcast_to(block[:, x : x + 1], (SUB, LANES))
                            for x in range(start, start + CHUNK)
                        ]
                    )
                    add(channel, part * near)
                add(channels, q1_ref[group, index, window] * weight)
                add(channels + 1, q2_ref[group, index, window] * weight)
            for channel in range(channels):
                d_ref[channel, row, window, :] = jnp.sum(totals[channel], axis=1)
            a_ref[row, window, :] = jnp.sum(totals[channels], axis=1)
            b_ref[row, window, :] = jnp.sum(totals[channels + 1], axis=1)
        return carry

    lax.fori_loop(0, ROWS, body, 0)

    @pl.when(step == SIDE // ROWS - 1)
    def _():
        square = second_ref[0] * second_ref[0]
        for channel in range(1, channels):
            square = square + second_ref[channel] * second_ref[channel]
        first_diag = plane_window(square * (1.0 / channels))
        energy, rate = self_energy(first_diag)
        second_diag = plane_window(energy)
        grad_two = b_ref[...] * (0.5 / (second_diag + JITTER))
        grad_one = a_ref[...] * (0.5 / (first_diag + JITTER)) + plane_window(grad_two) * rate
        a_ref[...] = plane_window(grad_one) * (2.0 / channels)
        strips = SIDE * SIDE // LANES
        rows = SIDE // strips
        for channel in range(channels):
            for strip in range(strips):
                window = slice(strip * rows, (strip + 1) * rows)
                value = d_ref[channel, window] + a_ref[window] * second_ref[channel, window]
                out_ref[channel * strips + strip] = value.reshape(LANES, LANES).T


def contract(weight, first, second, prod, q1, q2):
    channels, groups = first.shape[:2]
    big_spec = pl.BlockSpec((groups, ROWS, SIDE, SUB, LANES), lambda s: (0, s, 0, 0, 0))
    strips = channels * SIDE * SIDE // LANES
    return pl.pallas_call(
        contract_kernel,
        grid=(SIDE // ROWS,),
        out_shape=jax.ShapeDtypeStruct((strips, LANES, LANES), jnp.float32),
        in_specs=[
            pl.BlockSpec(weight.shape, lambda s: (0, 0, 0)),
            pl.BlockSpec(first.shape, lambda s: (0, 0, 0, 0, 0)),
            pl.BlockSpec(second.shape, lambda s: (0, 0, 0, 0)),
            big_spec, big_spec, big_spec,
        ],
        out_specs=pl.BlockSpec((strips, LANES, LANES), lambda s: (0, 0, 0)),
        scratch_shapes=[
            pltpu.VMEM((channels, SIDE, SIDE, LANES), jnp.float32),
            pltpu.VMEM((SIDE, SIDE, LANES), jnp.float32),
            pltpu.VMEM((SIDE, SIDE, LANES), jnp.float32),
        ],
        compiler_params=pltpu.CompilerParams(vmem_limit_bytes=50 * 1024 * 1024),
        name="contract",
    )(weight, first, second, prod, q1, q2)


def bits_of(row_count, col_count):
    rows = row_count.bit_length() - 1
    cols = col_count.bit_length() - 1
    order = [("row", 0)] if rows else []
    return order + [("col", k) for k in range(cols)] + [("row", k) for k in range(1, rows)]


def flip(index, bit):
    size = 1 << bit
    mine = lax.rem(lax.div(index, jnp.int32(size)), jnp.int32(2))
    return mine, index + size - 2 * size * mine


def partner_of(axis, bit):
    row, col = lax.axis_index("row"), lax.axis_index("col")
    if axis == "row":
        mine, row = flip(row, bit)
    else:
        mine, col = flip(col, bit)
    return mine, (row, col)


def greet(partners):
    barrier = pltpu.get_barrier_semaphore()
    for unused, device in partners:
        pl.semaphore_signal(barrier, inc=1, device_id=device, device_id_type=MESH)
    pl.semaphore_wait(barrier, len(partners))


def sum_kernel(bits, value_ref, out_ref, send_ref, recv_ref, send_sem, recv_sem):
    partners = [partner_of(*item) for item in bits]
    greet(partners)
    total = value_ref[...]
    for step, (unused, device) in enumerate(partners):
        send_ref[step] = total
        copy = pltpu.make_async_remote_copy(
            src_ref=send_ref.at[step], dst_ref=recv_ref.at[step],
            send_sem=send_sem.at[step], recv_sem=recv_sem.at[step],
            device_id=device, device_id_type=MESH,
        )
        copy.start()
        copy.wait()
        total = total + recv_ref[step]
    out_ref[...] = total


def sum_all(value, bits, collective):
    steps = len(bits)
    return pl.pallas_call(
        functools.partial(sum_kernel, bits),
        out_shape=jax.ShapeDtypeStruct(value.shape, value.dtype),
        in_specs=[pl.BlockSpec(memory_space=pltpu.VMEM)],
        out_specs=pl.BlockSpec(memory_space=pltpu.VMEM),
        scratch_shapes=[
            pltpu.VMEM((steps,) + value.shape, value.dtype),
            pltpu.VMEM((steps,) + value.shape, value.dtype),
            pltpu.SemaphoreType.DMA((steps,)),
            pltpu.SemaphoreType.DMA((steps,)),
        ],
        compiler_params=pltpu.CompilerParams(collective_id=collective, has_side_effects=True),
        name="sum_all",
    )(value)


def gather_kernel(bits, value_ref, out_ref, hold_ref, send_sem, recv_sem):
    partners = [partner_of(*item) for item in bits]
    greet(partners)
    place = 0
    for step, (mine, unused) in enumerate(partners):
        place = place + (mine << step)
    hold_ref[place] = value_ref[...]
    for step, (unused, device) in enumerate(partners):
        size = 1 << step
        window = pl.ds(lax.div(place, jnp.int32(size)) * size, size)
        copy = pltpu.make_async_remote_copy(
            src_ref=hold_ref.at[window], dst_ref=hold_ref.at[window],
            send_sem=send_sem.at[step], recv_sem=recv_sem.at[step],
            device_id=device, device_id_type=MESH,
        )
        copy.start()
        copy.wait()
    out_ref[...] = hold_ref[...]


def gather_all(value, bits, collective):
    steps = len(bits)
    shape = (1 << steps,) + value.shape
    return pl.pallas_call(
        functools.partial(gather_kernel, bits),
        out_shape=jax.ShapeDtypeStruct(shape, value.dtype),
        in_specs=[pl.BlockSpec(memory_space=pltpu.VMEM)],
        out_specs=pl.BlockSpec(memory_space=pltpu.VMEM),
        scratch_shapes=[
            pltpu.VMEM(shape, value.dtype),
            pltpu.SemaphoreType.DMA((steps,)),
            pltpu.SemaphoreType.DMA((steps,)),
        ],
        compiler_params=pltpu.CompilerParams(collective_id=collective, has_side_effects=True),
        name="gather_all",
    )(value)


def aligned(start):
    return start if isinstance(start, int) else pl.multiple_of(start, SUB)


CHUNKS = 2


def reduce_kernel(bits, value_ref, out_ref, hold_ref, recv_ref, back_ref, send_sem, recv_sem, back_send, back_recv):
    strips, support = value_ref.shape[:2]
    panel = back_ref.shape[1]
    steps = len(bits)
    partners = [partner_of(*item) for item in bits]
    greet(partners)
    chunks = [
        {"lead": strips // CHUNKS, "lead_at": k * (strips // CHUNKS), "size": support, "size_at": 0, "rel": 0, "undo": []}
        for k in range(CHUNKS)
    ]
    offset = [0]

    def begin(number, step):
        chunk = chunks[number]
        lead, size = chunk["lead"], chunk["size"]
        lead_at, size_at, rel = chunk["lead_at"], chunk["size_at"], chunk["rel"]
        axis = bits[step][0]
        mine, device = partners[step]
        wide = size > panel
        if axis == "col" or (not wide and (size // 2) % SUB == 0):
            half = size // 2
            keep_at, send_at = size_at + mine * half, size_at + (1 - mine) * half
            keep = (pl.ds(lead_at, lead), pl.ds(aligned(keep_at), half))
            send = (pl.ds(lead_at, lead), pl.ds(aligned(send_at), half))
            shape = (lead, half)
            chunk["size"], chunk["size_at"] = half, keep_at
            chunk["rel"] = rel + mine * half if axis == "row" else 0
        elif lead % 2 == 0:
            half = lead // 2
            keep_at, send_at = lead_at + mine * half, lead_at + (1 - mine) * half
            keep = (pl.ds(keep_at, half), pl.ds(aligned(size_at), size))
            send = (pl.ds(send_at, half), pl.ds(aligned(size_at), size))
            shape = (half, size)
            chunk["lead"], chunk["lead_at"] = half, keep_at
        else:
            keep = send = (pl.ds(lead_at, lead), pl.ds(aligned(size_at), size))
            shape = (lead, size)
        if axis == "row" and shape != (lead, size):
            extent = min(chunk["size"], panel)
            chunk["undo"].append(
                (device, (pl.ds(chunk["lead_at"], chunk["lead"]), pl.ds(aligned(chunk["rel"]), extent)))
            )
        land = (pl.ds(offset[0], shape[0]), pl.ds(0, shape[1]))
        offset[0] += shape[0]
        source = value_ref if step == 0 else hold_ref
        slot = number * steps + step
        copy = pltpu.make_async_remote_copy(
            src_ref=source.at[send], dst_ref=recv_ref.at[land],
            send_sem=send_sem.at[slot], recv_sem=recv_sem.at[slot],
            device_id=device, device_id_type=MESH,
        )
        copy.start()
        chunk["open"] = (copy, source, keep, land)

    def end(number):
        copy, source, keep, land = chunks[number]["open"]
        copy.wait()
        hold_ref[keep] = source[keep] + recv_ref[land]

    for step in range(steps):
        for number in range(CHUNKS):
            if step:
                end(number)
            begin(number, step)
    for number in range(CHUNKS):
        end(number)
        chunk = chunks[number]
        inner = (pl.ds(chunk["lead_at"], chunk["lead"]), pl.ds(aligned(chunk["rel"]), chunk["size"]))
        outer = (pl.ds(chunk["lead_at"], chunk["lead"]), pl.ds(aligned(chunk["size_at"]), chunk["size"]))
        back_ref[inner] = hold_ref[outer]
        chunk["copy"] = None
        chunk["undo"].reverse()
        undo(chunk, number * steps, 0, back_ref, back_send, back_recv)
    for step in range(1, len(chunks[0]["undo"])):
        for number in range(CHUNKS):
            chunks[number]["copy"].wait()
            undo(chunks[number], number * steps, step, back_ref, back_send, back_recv)
    for number in range(CHUNKS):
        if chunks[number]["copy"] is not None:
            chunks[number]["copy"].wait()
    out_ref[...] = back_ref[...]


def undo(chunk, base, step, back_ref, back_send, back_recv):
    if step >= len(chunk["undo"]):
        return
    device, window = chunk["undo"][step]
    chunk["copy"] = pltpu.make_async_remote_copy(
        src_ref=back_ref.at[window], dst_ref=back_ref.at[window],
        send_sem=back_send.at[base + step], recv_sem=back_recv.at[base + step],
        device_id=device, device_id_type=MESH,
    )
    chunk["copy"].start()


def reduce_panels(value, row_count, col_count, collective):
    strips, support = value.shape[:2]
    rows, cols = row_count.bit_length() - 1, col_count.bit_length() - 1
    bits = [("row", 0)] + [("col", k) for k in reversed(range(cols))] + [("row", k) for k in range(1, rows)]
    steps = len(bits)
    panel = support // col_count
    return pl.pallas_call(
        functools.partial(reduce_kernel, bits),
        out_shape=jax.ShapeDtypeStruct((strips, panel, LANES), value.dtype),
        in_specs=[pl.BlockSpec(memory_space=pltpu.VMEM)],
        out_specs=pl.BlockSpec(memory_space=pltpu.VMEM),
        scratch_shapes=[
            pltpu.VMEM(value.shape, value.dtype),
            pltpu.VMEM((strips * steps // 2, support, LANES), value.dtype),
            pltpu.VMEM((strips, panel, LANES), value.dtype),
            pltpu.SemaphoreType.DMA((CHUNKS * steps,)),
            pltpu.SemaphoreType.DMA((CHUNKS * steps,)),
            pltpu.SemaphoreType.DMA((CHUNKS * steps,)),
            pltpu.SemaphoreType.DMA((CHUNKS * steps,)),
        ],
        compiler_params=pltpu.CompilerParams(
            collective_id=collective, has_side_effects=True, vmem_limit_bytes=40 * 1024 * 1024
        ),
        name="reduce_panels",
    )(value)


def panels_kernel(cols, panel_ref, all_ref, second_ref, hold_ref, send_sem, recv_sem):
    strips, panel = panel_ref.shape[:2]
    half = strips // 2
    partners = [partner_of("col", k) for k in range(cols)] + [partner_of("row", 0)]
    greet(partners)
    col = lax.axis_index("col")
    mine = pl.ds(partners[-1][0] * half, half)
    hold_ref[mine, pl.ds(aligned(col * panel), panel)] = panel_ref[mine]
    for step, (unused, device) in enumerate(partners):
        window = (mine,)
        if step < cols:
            size = 1 << step
            start = lax.div(col, jnp.int32(size)) * (size * panel)
            window = (mine, pl.ds(aligned(start), size * panel))
        copy = pltpu.make_async_remote_copy(
            src_ref=hold_ref.at[window], dst_ref=hold_ref.at[window],
            send_sem=send_sem.at[step], recv_sem=recv_sem.at[step],
            device_id=device, device_id_type=MESH,
        )
        copy.start()
        copy.wait()

    def turn(strip, carry):
        block = hold_ref[strip]
        all_ref[strip] = block
        second_ref[strip] = block.T
        return carry

    lax.fori_loop(0, strips, turn, 0)


def gather_panels(panels, col_count, collective):
    strips, panel = panels.shape[:2]
    support = panel * col_count
    cols = col_count.bit_length() - 1
    return pl.pallas_call(
        functools.partial(panels_kernel, cols),
        out_shape=(
            jax.ShapeDtypeStruct((strips, support, LANES), panels.dtype),
            jax.ShapeDtypeStruct((strips, LANES, support), panels.dtype),
        ),
        in_specs=[pl.BlockSpec(memory_space=pltpu.VMEM)],
        out_specs=(pl.BlockSpec(memory_space=pltpu.VMEM), pl.BlockSpec(memory_space=pltpu.VMEM)),
        scratch_shapes=[
            pltpu.VMEM((strips, support, LANES), panels.dtype),
            pltpu.SemaphoreType.DMA((cols + 1,)),
            pltpu.SemaphoreType.DMA((cols + 1,)),
        ],
        compiler_params=pltpu.CompilerParams(
            collective_id=collective, has_side_effects=True, vmem_limit_bytes=24 * 1024 * 1024
        ),
        name="gather_panels",
    )(panels)


def exact_dot(left, right):
    return jnp.dot(left, right, precision=lax.Precision.HIGHEST, preferred_element_type=jnp.float32)


def solve_kernel(ss_ref, ts_ref, wanted_ref, labels_ref, inverse_ref, ridged_ref, alphas_ref, residual_ref, message_ref):
    number = ss_ref.shape[0]
    rows = lax.broadcasted_iota(jnp.int32, (number, number), 0)
    lanes = lax.broadcasted_iota(jnp.int32, (number, number), 1)
    kernel = ss_ref[...]
    trace = jnp.sum(jnp.where(rows == lanes, kernel, 0.0))
    ridged = kernel + jnp.where(rows == lanes, RIDGE * trace / number, 0.0)
    ridged_ref[...] = ridged
    lane = lax.broadcasted_iota(jnp.int32, (SUB, number), 1)
    sublane = lax.broadcasted_iota(jnp.int32, (SUB, number), 0)
    blocks = [ridged[k : k + SUB] for k in range(0, number, SUB)]
    for k in range(number):
        home, inner = divmod(k, SUB)
        row = blocks[home][inner : inner + 1]
        line = jnp.where(lane[:1] == k, 1.0, row) * (1.0 / row[:, k : k + 1])
        here = lane == k
        blocks = [jnp.where(here, 0.0, block) - block[:, k : k + 1] * line for block in blocks]
        blocks[home] = jnp.where(sublane == inner, line, blocks[home])
    inverse = jnp.concatenate(blocks, axis=0)
    inverse_ref[...] = inverse
    labels = labels_ref[...]
    alphas = exact_dot(inverse, labels)
    alphas = alphas + exact_dot(inverse, labels - exact_dot(ridged, alphas))
    alphas_ref[...] = alphas
    residual = exact_dot(ts_ref[...], alphas) - wanted_ref[...]
    residual_ref[...] = residual
    partial = lax.dot_general(
        residual, ts_ref[...], (((0,), (0,)), ((), ())),
        precision=lax.Precision.HIGHEST, preferred_element_type=jnp.float32,
    )
    classes = residual.shape[1]
    spare = message_ref.shape[0] - classes
    squared = jnp.sum(residual * residual)
    message_ref[...] = jnp.concatenate([partial, jnp.broadcast_to(squared, (spare, number))], axis=0)


def solve(kernel_ss, kernel_ts, wanted, labels):
    number, classes = labels.shape
    targets = kernel_ts.shape[0]
    tall = -(-(classes + 1) // SUB) * SUB
    shapes = [(number, number), (number, number), (number, classes), (targets, classes), (tall, number)]
    return pl.pallas_call(
        solve_kernel,
        out_shape=tuple(jax.ShapeDtypeStruct(shape, jnp.float32) for shape in shapes),
        compiler_params=pltpu.CompilerParams(vmem_limit_bytes=16 * 1024 * 1024),
        name="solve",
    )(kernel_ss, kernel_ts, wanted, labels)


def order_matrix(panel_order, blocks):
    return (panel_order[:, None] == jnp.arange(blocks, dtype=jnp.int32)[None, :]).astype(
        jnp.float32
    )


def local(target_images, target_labels, support_images, support_labels, panel_order):
    highest = lax.Precision.HIGHEST
    row_count = lax.axis_size("row")
    col_count = lax.axis_size("col")
    devices = row_count * col_count
    panel_size, channels, pixels = support_images.shape
    support = panel_size * col_count
    targets_dev = target_images.shape[0]
    bits = bits_of(row_count, col_count)
    place = 0
    for step, (axis, bit) in enumerate(bits):
        place = place + (((lax.axis_index(axis) >> bit) & 1) << step)

    strips = channels * pixels // LANES
    panels = support_images.reshape(panel_size, strips, LANES).transpose(1, 0, 2)
    gathered, second = gather_panels(panels, col_count, 0)
    second = second.reshape(channels, SIDE, SIDE, support)
    own_rows = -(-support // devices)
    owners = support // own_rows
    own_start = lax.rem(place, owners) * own_rows
    own = lax.dynamic_slice_in_dim(gathered, own_start, own_rows, 1)
    own = own.transpose(1, 0, 2).reshape(own_rows, channels, pixels)
    count = targets_dev + own_rows
    groups = -(-count // SUB)
    first = jnp.concatenate([target_images, own], axis=0)
    first = jnp.pad(first, ((0, groups * SUB - count), (0, 0), (0, 0)))
    first = first.reshape(groups, SUB, channels, SIDE, SIDE).transpose(2, 0, 3, 1, 4)
    first = jnp.pad(first, ((0, 0),) * 4 + ((0, LANES - SIDE),))

    values, prod, q1, q2 = pair_maps(first, second)
    values = values.reshape(groups * SUB, support)
    kernel_ts = values[:targets_dev]
    mine = values[targets_dev:count]
    block = jnp.pad(mine, ((0, -own_rows % SUB), (0, 0)))
    kernel_ss = gather_all(block, bits, 1)[:owners, :own_rows].reshape(support, support)

    wanted = (target_labels[:, None] == jnp.arange(CLASSES, dtype=jnp.int32)[None, :]).astype(
        jnp.float32
    ) - 0.1
    matrix = order_matrix(panel_order, support)
    stored_labels = jnp.dot(matrix, support_labels, precision=highest)
    inverse, ridged, alphas, residual, message = solve(kernel_ss, kernel_ts, wanted, stored_labels)
    summed = sum_all(message, bits, 2)
    alpha_grad = summed[:CLASSES].T
    total_targets = targets_dev * devices
    loss_value = 0.5 * summed[CLASSES, 0] / total_targets
    adjoint = jnp.dot(inverse, alpha_grad, precision=highest)
    missing = alpha_grad - jnp.dot(ridged, adjoint, precision=highest)
    adjoint = adjoint + jnp.dot(inverse, missing, precision=highest)
    own_alphas = lax.dynamic_slice_in_dim(alphas, own_start, own_rows, 0)
    own_adjoint = lax.dynamic_slice_in_dim(adjoint, own_start, own_rows, 0)
    ids = own_start + jnp.arange(own_rows, dtype=jnp.int32)
    diagonal = (ids[:, None] == jnp.arange(support, dtype=jnp.int32)[None, :]).astype(jnp.float32)
    kss_grad = (
        -jnp.dot(own_adjoint, alphas.T, precision=highest)
        - jnp.dot(own_alphas, adjoint.T, precision=highest)
        - 2.0 * RIDGE / support * jnp.sum(adjoint * alphas) * diagonal
    )
    kss_grad = jnp.where(place < owners, kss_grad, 0.0)
    kts_grad = jnp.dot(residual, alphas.T, precision=highest)
    weight = jnp.concatenate([kts_grad, kss_grad], axis=0) * (1.0 / pixels)
    weight = jnp.pad(weight, ((0, groups * SUB - count), (0, 0))).reshape(groups, SUB, support)

    gradient = contract(weight, first, second, prod, q1, q2)
    panel = reduce_panels(gradient, row_count, col_count, 3)
    grad_support = (
        panel.reshape(channels, pixels // LANES, panel_size, LANES)
        .transpose(2, 0, 1, 3)
        .reshape(panel_size, channels, pixels)
    )
    return (loss_value, grad_support, jnp.dot(matrix.T, adjoint, precision=highest))


def solution(mesh):
    placed = (P(("row", "col"), None, None), P(("row", "col")), P("col", None, None), P(), P())
    return jax.shard_map(
        local,
        mesh=mesh,
        in_specs=placed,
        out_specs=(P(), P("col", None, None), P()),
        check_vma=False,
    )
```
